256 devices in a mesh: pat: 32 (over x, y, z_hi), code: 8 (over z_lo, core).
Axes of the slice: x: 4, y: 4, z: 8 (z_hi: 2, z_lo: 4; z = z_hi * 4 + z_lo), core: 2. Of those that a mesh axis runs over, the one named last changes fastest.
Arguments:
- tiles: bfloat16 [768, 128, 120, 128], P(('pat', 'code')), may hold values from 0 to 32
- patient_block: int32 [768], P(('pat', 'code')), may hold values from 0 to 3
- owner: int32 [768, 1], P(('pat', 'code')), may hold values from 0 to 31
- sub_block: int32 [768], P(('pat', 'code')), may hold values from 0 to 1
- live: int32 [768], P(('pat', 'code')), may hold values 0 or 1
- code_factor: bfloat16 [65536, 256], P(('pat', 'code')), may hold values from -0.00390625 to 0.01171875
- month_factor: float32 [120, 256], replicated, may hold values from -0.0913 to 0.2739
Outputs:
- patient_factor: float32 [16384, 256], P(('pat', 'code'))
The draws below stay inside these ranges and needn't reach their ends.
All inputs are finite; a program needn't handle non-finite values. No bound on the sum of `live` on one device may be relied on, other than what follows from the above.
Results may differ from the reference program's by a relative error of at most 0.0003.
Values may be sent and summed in bfloat16 or wider, within the bound.
A program may use at most 128 MiB of HBM per device.

```python
import jax
import jax.numpy as jnp
from jax import lax

CODES = 65536
RANK = 256
MONTHS = 120
BLOCK = 128
TILES = 3
PATB = 4
OWN = 2
SLOTS = 768
N_PAT = 32
N_CODE = 8


def plant(result, rng, least, top_value):
    shape = result.shape
    place = [jax.random.randint(jax.random.fold_in(rng, axis), (), 0, shape[axis]) for axis in range(len(shape))]
    result = result.at[tuple(place)].set(least)
    longest = shape.index(max(shape))
    place[longest] = (place[longest] + 1) % shape[longest]
    return result.at[tuple(place)].set(top_value)


def level_of(stream_key, extent, cuts, low, top_value):
    def one(axis_at, blocks):
        draws = jax.random.uniform(jax.random.fold_in(jax.random.fold_in(stream_key, 6), axis_at), (blocks,), jnp.float32, low / len(cuts), top_value / len(cuts))
        return jnp.repeat(jnp.exp(draws), extent[axis_at] // blocks).reshape((-1,) + (1,) * (len(extent) - axis_at - 1))

    loudness = one(*cuts[0])
    for cut in cuts[1:]:
        loudness = loudness * one(*cut)
    return loudness


def setup_inputs(seed: int = 0) -> dict:
    keys = jax.random.split(jax.random.key(seed), 8)
    tiles = jnp.clip(32.0 * jax.random.uniform(keys[0], (SLOTS, BLOCK, MONTHS, BLOCK), jnp.float32) ** level_of(keys[0], (SLOTS, BLOCK, MONTHS, BLOCK), ((0, 256),), -0.2, 0.2), 0.0, 32.0).astype(jnp.bfloat16)
    patient_block = plant(jax.random.randint(keys[1], (SLOTS,), 0, PATB), jax.random.fold_in(keys[1], 1), 0, PATB - 1).astype(jnp.int32)
    owner = plant(jax.random.randint(keys[2], (SLOTS, 1), 0, N_PAT), jax.random.fold_in(keys[2], 1), 0, N_PAT - 1).astype(jnp.int32)
    sub_block = plant(jax.random.randint(keys[3], (SLOTS,), 0, OWN), jax.random.fold_in(keys[3], 1), 0, OWN - 1).astype(jnp.int32)
    live = plant((jax.random.randint(keys[4], (SLOTS,), 0, 8) < 7).astype(jnp.int32), jax.random.fold_in(keys[4], 1), 0, 1)
    code_factor = jnp.clip(-0.00390625 + 0.015625 * jax.random.uniform(keys[5], (CODES, RANK), jnp.float32) ** level_of(keys[5], (CODES, RANK), ((0, 256),), -0.2, 0.2), -0.00390625, 0.01171875).astype(jnp.bfloat16)
    month_factor = jnp.clip(jax.random.uniform(keys[6], (MONTHS, RANK), jnp.float32, -0.0913, 0.2739), -0.0913, 0.2739)
    return dict(tiles=tiles, patient_block=patient_block, owner=owner, sub_block=sub_block, live=live, code_factor=code_factor, month_factor=month_factor)


def reference(tiles, patient_block, owner, sub_block, live, code_factor, month_factor):
    count = tiles.shape[0]
    own = CODES // (N_PAT * N_CODE * BLOCK)
    slot = jnp.arange(count, dtype=jnp.int32)
    device = slot // TILES
    code_index = device % N_CODE
    pat_index = device // N_CODE
    code_row = (((owner[:, 0] * N_CODE + code_index) * own + sub_block) * BLOCK).astype(jnp.int32)
    block_id = (pat_index * PATB + patient_block).astype(jnp.int32)

    def single(items):
        tile, row, flag = items
        block = lax.dynamic_slice_in_dim(code_factor, row, BLOCK, 0)
        wide = jnp.dot(tile.reshape(BLOCK * MONTHS, BLOCK).astype(jnp.float32), block.astype(jnp.float32), preferred_element_type=jnp.float32)
        wide = wide.reshape(BLOCK, MONTHS, RANK)
        return jnp.sum(wide * month_factor[None], axis=1) * flag.astype(jnp.float32)
    parts = lax.map(single, (tiles, code_row, live))
    mttkrp = jax.ops.segment_sum(parts, block_id, num_segments=N_PAT * PATB).reshape(N_PAT * PATB * BLOCK, RANK)
    code_gram = jnp.dot(code_factor.T.astype(jnp.float32), code_factor.astype(jnp.float32), preferred_element_type=jnp.float32)
    month_gram = jnp.dot(month_factor.T.astype(jnp.float32), month_factor.astype(jnp.float32), precision=lax.Precision.HIGHEST, preferred_element_type=jnp.float32)
    gram = code_gram * month_gram
    lower = jnp.linalg.cholesky(gram)
    return jax.scipy.linalg.cho_solve((lower, True), mttkrp.T).T
```

```python
import jax
import jax.numpy as jnp
from jax import lax
from jax.experimental import pallas as pl
from jax.experimental.pallas import tpu as pltpu
from jax.sharding import PartitionSpec as P

MESH = pl.DeviceIdType.MESH
HI = lax.Precision.HIGHEST
F32 = jnp.float32
BLOCK = 128
MONTHS = 120
RANK = 256
SLOTS = 3
HALF = 64
CHUNK = 32
SIDE = 64


def recip(p):
    r = pltpu.reciprocal(p, approx=True)
    r = r * (2.0 - p * r)
    return r * (2.0 - p * r)


def sweep(x, n):
    rows = lax.broadcasted_iota(jnp.int32, x.shape, 0)
    cols = lax.broadcasted_iota(jnp.int32, x.shape, 1)
    for k in range(n):
        row, col = x[k : k + 1, :], x[:, k : k + 1]
        inv = recip(x[k : k + 1, k : k + 1])
        w = row * inv
        y = x - col * w
        y = jnp.where(cols == k, col * inv, y)
        x = jnp.where(rows == k, jnp.where(cols == k, -inv, w), y)
    return x


def negative_inverse(a):
    for o in range(0, RANK, SIDE):
        small = sweep(a[o : o + SIDE, o : o + SIDE], SIDE)
        rows = a[o : o + SIDE, :]
        w = -jnp.dot(small, rows, precision=HI, preferred_element_type=F32)
        u = lax.dot_general(
            rows, w, (((0,), (0,)), ((), ())), precision=HI, preferred_element_type=F32
        )
        a[...] = a[...] - u
        a[o : o + SIDE, :] = w
        a[:, o : o + SIDE] = w.T
        a[o : o + SIDE, o : o + SIDE] = small


def kernel(
    owner, sub, block_at, live, tiles, code, month, out,
    counts, group, gram_own, plane_in, piece, column_in, whole, gram, month_gram,
    part, pair_in, line_out, line_in,
    tile_sem, zh_s, zh_r, first_s, first_r, second_s, second_r,
    plane_s, plane_r, column_s, column_r, spread_s, spread_r,
    pair_s, pair_r, line_s, line_r,
):
    pat, code_at = lax.axis_index("pat"), lax.axis_index("code")
    x, y, zh = pat // 8, (pat // 2) % 4, pat % 2
    zl, core = code_at // 2, code_at % 2
    z = zh * 4 + zl

    def device(x, y, z, c):
        x, y, z = lax.rem(x, 4), lax.rem(y, 4), lax.rem(z, 8)
        return ((x * 4 + y) * 2 + z // 4, lax.rem(z, 4) * 2 + c)

    def plane(e):
        px, py, pc = lax.rem(x + e // 8, 4), lax.rem(y + (e // 2) % 4, 4), lax.rem(core + e % 2, 2)
        return device(px, py, z, pc), (px * 4 + py) * 2 + pc

    def remote(src, dst, send, recv, to):
        return pltpu.make_async_remote_copy(
            src_ref=src, dst_ref=dst, send_sem=send, recv_sem=recv, device_id=to, device_id_type=MESH
        )

    loads = [
        pltpu.make_async_copy(tiles.at[k], counts.at[k], tile_sem.at[k]) for k in range(SLOTS)
    ]
    for load in loads:
        load.start()

    barrier = pltpu.get_barrier_semaphore()

    def greet(e, _):
        pl.semaphore_signal(barrier, inc=1, device_id=plane(e)[0], device_id_type=MESH)
        return 0

    lax.fori_loop(1, 32, greet, 0)
    for d in range(1, 8):
        pl.semaphore_signal(
            barrier, inc=1, device_id=device(x, y, z + d, core), device_id_type=MESH
        )
    own = lax.dot_general(
        code[...], code[...], (((0,), (0,)), ((), ())), preferred_element_type=F32
    )
    gram_own[...] = own.reshape(32, 8, RANK)
    uv = [(x, y), (y, x)]
    for h in range(2):
        u, v = uv[h]
        group[h, zh, v, u] = code[h * BLOCK : (h + 1) * BLOCK, :]
    pl.semaphore_wait(barrier, 38)

    def first_stage(s, who):
        copies = []
        for h in range(2):
            u, v = uv[h]
            for d in range(1, 4):
                to = device(x + d, y, z, core) if h == 0 else device(x, y + d, z, core)
                here = group.at[h, who, v, u]
                copies.append(
                    remote(here, here, first_s.at[s, h, d - 1], first_r.at[s, h, d - 1], to)
                )
        for c in copies:
            c.start()
        return copies

    def second_stage(s, who):
        copies = []
        for h in range(2):
            u, v = uv[h]
            for d in range(1, 4):
                to = device(x, y + d, z, core) if h == 0 else device(x + d, y, z, core)
                here = group.at[h, who, v]
                copies.append(
                    remote(here, here, second_s.at[s, h, d - 1], second_r.at[s, h, d - 1], to)
                )
        for c in copies:
            c.start()
        return copies

    me = (x * 4 + y) * 2 + core

    def scatter(e, _):
        to, q = plane(e)
        remote(gram_own.at[q], plane_in.at[e - 1], plane_s, plane_r, to).start()
        return 0

    lax.fori_loop(1, 32, scatter, 0)
    first_own = first_stage(0, zh)

    def arrived(buf, sem):
        pltpu.make_async_copy(buf, buf, sem).wait()

    month_gram[...] = lax.dot_general(
        month[...], month[...], (((0,), (0,)), ((), ())), precision=HI, preferred_element_type=F32
    )
    arrived(plane_in, plane_r)
    total = gram_own[me]
    for e in range(31):
        total = total + plane_in[e]
    piece[0] = total
    columns = []
    for d in range(1, 8):
        columns.append(
            remote(
                piece.at[0], column_in.at[d - 1], column_s.at[d - 1], column_r.at[d - 1],
                device(x, y, z + d, core),
            )
        )
    for c in columns:
        c.start()
    across = []
    for h in range(2):
        u, v = uv[h]
        across.append(
            remote(
                code.at[h * BLOCK : (h + 1) * BLOCK, :], group.at[h, zh, v, u],
                zh_s.at[h], zh_r.at[h], device(x, y, z + 4, core),
            )
        )
    for c in across:
        c.start()
    for c in first_own:
        c.wait()
    second_own = second_stage(0, zh)
    for c in columns:
        c.wait()
    total = piece[0]
    for d in range(7):
        total = total + column_in[d]
    piece[1] = total
    whole[me] = total

    def spread(e, _):
        to, _q = plane(e)
        remote(piece.at[1], whole.at[me], spread_s, spread_r, to).start()
        return 0

    lax.fori_loop(1, 32, spread, 0)
    for c in across:
        c.wait()
    first_other = first_stage(1, 1 - zh)
    arrived(whole.at[0:31], spread_r)
    gram[...] = whole[...].reshape(RANK, RANK) * month_gram[...]
    for c in first_other:
        c.wait()
    second_other = second_stage(1, 1 - zh)
    negative_inverse(gram)
    for c in second_own + second_other:
        c.wait()
    for load in loads:
        load.wait()

    blocks = []
    for k in range(SLOTS):
        o, s = owner[k], sub[k]
        ox, oy, oz = o // 8, (o // 2) % 4, o % 2
        ou, ov = jnp.where(s == 0, ox, oy), jnp.where(s == 0, oy, ox)
        blocks.append((s, oz, ov, ou))

    def contract(p):
        pieces = []
        for k in range(SLOTS):
            lhs = counts[k, pl.ds(pl.multiple_of(p * MONTHS, CHUNK * MONTHS), CHUNK * MONTHS), :]
            wide = jnp.dot(lhs, group[blocks[k]], preferred_element_type=F32)
            wide = wide.reshape(CHUNK, MONTHS, RANK) * month[...][None]
            pieces.append(jnp.sum(wide, axis=1) * live[k].astype(F32))
        return pieces

    for which in range(2):
        half = 1 - core if which == 0 else core

        def step(i, _, half=half):
            pieces = contract(half * HALF + i * CHUNK)
            for b in range(4):
                total = jnp.zeros((CHUNK, RANK), F32)
                for k in range(SLOTS):
                    total = total + jnp.where(block_at[k] == b, pieces[k], 0.0)
                part[half, b, pl.ds(pl.multiple_of(i * CHUNK, CHUNK), CHUNK), :] = total
            return 0

        lax.fori_loop(0, HALF // CHUNK, step, 0)
        if which == 0:
            pair = remote(
                part.at[1 - core], pair_in, pair_s, pair_r, device(x, y, z, 1 - core)
            )
            pair.start()
    pair.wait()
    line_out[...] = part[core] + pair_in[...]
    line = []
    for d in range(1, 4):
        zt = lax.rem(zl + d, 4)
        line.append(
            remote(
                line_out.at[zt], line_in.at[d - 1], line_s.at[d - 1], line_r.at[d - 1],
                device(x, y, zh * 4 + zt, core),
            )
        )
    for c in line:
        c.start()
    for c in line:
        c.wait()
    share = line_out[zl] + line_in[0] + line_in[1] + line_in[2]
    out[...] = -jnp.dot(share, gram[...], precision=HI, preferred_element_type=F32)
    arrived(gram_own.at[0:31], plane_s)
    arrived(gram_own.at[0:31], spread_s)


def local(tiles, patient_block, owner, sub_block, live, code_factor, month_factor):
    dma, vmem = pltpu.SemaphoreType.DMA, pltpu.VMEM
    smem_spec = pl.BlockSpec(memory_space=pltpu.SMEM)
    vmem_spec = pl.BlockSpec(memory_space=pltpu.VMEM)
    return pl.pallas_call(
        kernel,
        out_shape=jax.ShapeDtypeStruct((HALF, RANK), F32),
        in_specs=[smem_spec] * 4 + [pl.BlockSpec(memory_space=pl.ANY), vmem_spec, vmem_spec],
        out_specs=vmem_spec,
        scratch_shapes=[
            vmem((SLOTS, BLOCK * MONTHS, BLOCK), jnp.bfloat16),
            vmem((2, 2, 4, 4, BLOCK, RANK), jnp.bfloat16),
            vmem((32, 8, RANK), F32),
            vmem((31, 8, RANK), F32),
            vmem((2, 8, RANK), F32),
            vmem((7, 8, RANK), F32),
            vmem((32, 8, RANK), F32),
            vmem((RANK, RANK), F32),
            vmem((RANK, RANK), F32),
            vmem((2, 4, HALF, RANK), F32),
            vmem((4, HALF, RANK), F32),
            vmem((4, HALF, RANK), F32),
            vmem((3, HALF, RANK), F32),
            dma((SLOTS,)),
            dma((2,)),
            dma((2,)),
            dma((2, 2, 3)),
            dma((2, 2, 3)),
            dma((2, 2, 3)),
            dma((2, 2, 3)),
            dma,
            dma,
            dma((7,)),
            dma((7,)),
            dma,
            dma,
            dma,
            dma,
            dma((3,)),
            dma((3,)),
        ],
        compiler_params=pltpu.CompilerParams(
            collective_id=0, has_side_effects=True, vmem_limit_bytes=56 << 20
        ),
        cost_estimate=pl.CostEstimate(
            flops=3_300_000_000, bytes_accessed=12_000_000, transcendentals=0
        ),
    )(
        owner.reshape(SLOTS),
        sub_block,
        patient_block,
        live,
        tiles.reshape(SLOTS, BLOCK * MONTHS, BLOCK),
        code_factor,
        month_factor,
    )


def solution(mesh):
    placed = (
        P(("pat", "code"), None, None, None),
        P(("pat", "code")),
        P(("pat", "code"), None),
        P(("pat", "code")),
        P(("pat", "code")),
        P(("pat", "code"), None),
        P(),
    )
    return jax.shard_map(
        local, mesh=mesh, in_specs=placed, out_specs=P(("pat", "code"), None), check_vma=False
    )
```

```python
import jax
import jax.numpy as jnp
from jax import lax
from jax.experimental import pallas as pl
from jax.experimental.pallas import tpu as pltpu
from jax.sharding import PartitionSpec as P

MESH = pl.DeviceIdType.MESH
HI = lax.Precision.HIGHEST
F32 = jnp.float32
BLOCK = 128
MONTHS = 120
RANK = 256
SLOTS = 3
HALF = 64
CHUNK = 32
SIDE = 32


def recip(p):
    r = pltpu.reciprocal(p, approx=True)
    return r * (2.0 - p * r)


def tree(values, bits):
    while len(values) > 1:
        values = [
            jnp.where(bits[0], values[i + 1], values[i]) for i in range(0, len(values), 2)
        ]
        bits = bits[1:]
    return values[0]


def add_up(values):
    while len(values) > 1:
        values = [values[i] + values[i + 1] for i in range(0, len(values), 2)]
    return values[0]


def lane_of(v, at):
    return jnp.broadcast_to(v[:, at : at + 1], (8, 128))


def row_of(v, at):
    return jnp.broadcast_to(v[at : at + 1, :], (8, 128))


def sweep_pairs(d):
    n = 8

    def at(i, j):
        return d[min(i, j), max(i, j)]

    for k in range(0, n, 2):
        a, b, c = at(k, k), at(k, k + 1), at(k + 1, k + 1)
        r = recip(a * c - b * b)
        ia, ib, ic = c * r, b * r, a * r
        rest = [i for i in range(n) if i > k + 1] + [i for i in range(n) if i < k]
        u = {
            i: (ia * at(k, i) - ib * at(k + 1, i), ic * at(k + 1, i) - ib * at(k, i)) for i in rest
        }
        new = {}
        for p, i in enumerate(rest):
            for j in rest[p:]:
                new[min(i, j), max(i, j)] = at(i, j) - (at(k, i) * u[j][0] + at(k + 1, i) * u[j][1])
        for i in rest:
            new[min(i, k), max(i, k)] = u[i][0]
            new[min(i, k + 1), max(i, k + 1)] = u[i][1]
        new[k, k], new[k, k + 1], new[k + 1, k + 1] = -ia, ib, -ic
        d = new
    return d


def panel(rows, half, l0, row, lane):
    c = [lane_of(rows[half], l0 + m) for m in range(8)]
    lines = [[row_of(rows[h], m) for m in range(8)] for h in range(2)]
    d = sweep_pairs({(i, j): row_of(c[j], i) for i in range(8) for j in range(i, 8)})
    row_bits = [(row & b) == b for b in (1, 2, 4)]
    rel = lane - l0
    lane_bits = [(rel & b) == b for b in (1, 2, 4)]
    minus = [tree([d[min(i, m), max(i, m)] for i in range(8)], row_bits) for m in range(8)]
    inside = -tree(minus, lane_bits)
    out = []
    for h in range(2):
        w = -add_up([minus[m] * lines[h][m] for m in range(8)])
        out.append(jnp.where((rel >= 0) & (rel < 8), inside, w) if h == half else w)
    return out


def turned_dot(a, b):
    return lax.dot_general(
        a, b, (((0,), (0,)), ((), ())), precision=HI, preferred_element_type=F32
    )


def clear_and_subtract(a, s, rows, done):
    wide = lax.broadcasted_iota(jnp.int32, (1, RANK), 1)
    o = s * SIDE
    inside = (wide >= o) & (wide < o + SIDE)
    a[...] = jnp.where(inside, 0.0, a[...]) - turned_dot(rows, done)
    a[pl.ds(pl.multiple_of(jnp.maximum(o, 0), SIDE), SIDE), :] = done


def eliminate(a, first, last, carry):
    row = lax.broadcasted_iota(jnp.int32, (8, 128), 0)
    lane = lax.broadcasted_iota(jnp.int32, (8, 128), 1)
    wide = lax.broadcasted_iota(jnp.int32, (1, RANK), 1)
    n = SIDE // 8

    def step(s, carry):
        turned, before, after = carry
        clear_and_subtract(a, s - 1, before, after)
        o = pl.multiple_of(s * SIDE, SIDE)
        ahead = pl.multiple_of(lax.rem(o + SIDE, RANK), SIDE)
        following = pltpu.roll(a[pl.ds(ahead, SIDE), :], RANK - o, 1)
        straight = pltpu.roll(turned, o, 1)
        rows = [[turned[8 * j : 8 * j + 8, :128], turned[8 * j : 8 * j + 8, 128:]] for j in range(n)]
        for j in range(n):
            l0 = 8 * j
            order = list(range(j + 1, n)) + list(range(j))
            factor = {i: [lane_of(rows[i][0], l0 + m) for m in range(8)] for i in order}
            rows[j] = panel(rows[j], 0, l0, row, lane)
            inside = (lane >= l0) & (lane < l0 + 8)
            w = [[row_of(rows[j][h], m) for m in range(8)] for h in range(2)]
            for i in order:
                for h in range(2):
                    old = jnp.where(inside, 0.0, rows[i][h]) if h == 0 else rows[i][h]
                    rows[i][h] = old - add_up([factor[i][m] * w[h][m] for m in range(8)])
        done = jnp.concatenate([jnp.concatenate(r, axis=1) for r in rows], axis=0)
        done = jnp.where(wide < SIDE, -done, done)
        following = jnp.where(wide < SIDE, 0.0, following) - turned_dot(
            turned[:, SIDE : 2 * SIDE], done
        )
        return pltpu.roll(following, RANK - SIDE, 1), straight, pltpu.roll(done, o, 1)

    return lax.fori_loop(first, last, step, carry)


def kernel(
    owner, sub, block_at, live, tiles, code_in, month_in, out,
    counts, code, month, group, need, need_in, asked, wanted, chosen, blocks,
    gram_own, plane_in, piece, column_in, whole, gram, month_gram,
    part, pair_in, line_out, line_in,
    tile_sem, small_sem, need_s, need_r, asked_sem, zh_s, zh_r, row_s, row_r, pick_s, pick_r,
    plane_s, plane_r, column_s, column_r, spread_s, spread_r,
    pair_s, pair_r, line_s, line_r,
):
    pat, code_at = lax.axis_index("pat"), lax.axis_index("code")
    x, y, zh = pat // 8, (pat // 2) % 4, pat % 2
    zl, core = code_at // 2, code_at % 2
    z = zh * 4 + zl
    me = (x * 4 + y) * 2 + core

    def device(x, y, z, c):
        x, y, z = lax.rem(x, 4), lax.rem(y, 4), lax.rem(z, 8)
        return ((x * 4 + y) * 2 + z // 4, lax.rem(z, 4) * 2 + c)

    def plane(e):
        px, py, pc = lax.rem(x + e // 8, 4), lax.rem(y + (e // 2) % 4, 4), lax.rem(core + e % 2, 2)
        return device(px, py, z, pc), (px * 4 + py) * 2 + pc

    def beside(h, d):
        return device(x + d, y, z, core) if h == 0 else device(x, y + d, z, core)

    def remote(src, dst, send, recv, to):
        return pltpu.make_async_remote_copy(
            src_ref=src, dst_ref=dst, send_sem=send, recv_sem=recv, device_id=to, device_id_type=MESH
        )

    def start(copies):
        for c in copies:
            c.start()
        return copies

    def arrived(buf, sem):
        pltpu.make_async_copy(buf, buf, sem).wait()

    small = start(
        [
            pltpu.make_async_copy(code_in, code, small_sem.at[0]),
            pltpu.make_async_copy(month_in, month, small_sem.at[1]),
        ]
    )
    loads = start(
        [pltpu.make_async_copy(tiles.at[k], counts.at[k], tile_sem.at[k]) for k in range(SLOTS)]
    )
    barrier = pltpu.get_barrier_semaphore()

    def greet(e, _):
        pl.semaphore_signal(barrier, inc=1, device_id=plane(e)[0], device_id_type=MESH)
        return 0

    lax.fori_loop(1, 32, greet, 0)
    for d in range(1, 8):
        pl.semaphore_signal(
            barrier, inc=1, device_id=device(x, y, z + d, core), device_id_type=MESH
        )
    line_at = lax.broadcasted_iota(jnp.int32, (8, 128), 0)
    places, away = [], []
    for k in range(SLOTS):
        o = owner[k]
        ox, oy, oz = o // 8, (o // 2) % 4, o % 2
        places.append([(oz * 4 + ox) * 2 + sub[k], (oz * 4 + oy) * 2 + sub[k]])
        away.append([lax.rem(y + 4 - oy, 4), lax.rem(x + 4 - ox, 4)])
    wish = jnp.zeros((8, 128), jnp.int32)
    for k in range(SLOTS):
        for h in range(2):
            wish = jnp.where(line_at == 2 * k + h, places[k][h], wish)
    need[...] = wish
    mine = [(zh * 4 + x) * 2, (zh * 4 + y) * 2]
    theirs = [((1 - zh) * 4 + x) * 2, ((1 - zh) * 4 + y) * 2]
    small[0].wait()
    for h in range(2):
        for b in range(2):
            group[h, mine[h] + b] = code[b * BLOCK : (b + 1) * BLOCK, h * BLOCK : (h + 1) * BLOCK]
    own = lax.dot_general(
        code[...], code[...], (((0,), (0,)), ((), ())), preferred_element_type=F32
    )
    gram_own[...] = own.reshape(32, 8, RANK)
    pl.semaphore_wait(barrier, 38)

    across = []
    for h in range(2):
        here = group.at[h, pl.ds(mine[h], 2)]
        across.append(remote(here, here, zh_s.at[h], zh_r.at[h], device(x, y, z + 4, core)))
    start(across)
    needs = start(
        [
            remote(need, need_in.at[h, d - 1], need_s.at[h, d - 1], need_r.at[h, d - 1], beside(1 - h, d))
            for h in range(2)
            for d in range(1, 4)
        ]
    )

    def scatter(e, _):
        to, q = plane(e)
        remote(gram_own.at[q], plane_in.at[e - 1], plane_s, plane_r, to).start()
        return 0

    lax.fori_loop(1, 32, scatter, 0)

    def along_line(s, first):
        copies = []
        for h in range(2):
            here = group.at[h, pl.ds(first[h], 2)]
            for d in range(1, 4):
                copies.append(
                    remote(here, here, row_s.at[s, h, d - 1], row_r.at[s, h, d - 1], beside(h, d))
                )
        return start(copies)

    row_copies = along_line(0, mine)
    small[1].wait()
    month_gram[...] = turned_dot(month[...], month[...])
    for c in needs:
        c.wait()
    to_scalars = pltpu.make_async_copy(need_in, asked, asked_sem)
    to_scalars.start()
    to_scalars.wait()
    arrived(plane_in, plane_r)

    def add_plane(e, total):
        return total + plane_in[e]

    piece[0] = lax.fori_loop(0, 31, add_plane, gram_own[me], unroll=True)
    columns = start(
        [
            remote(
                piece.at[0], column_in.at[d - 1], column_s.at[d - 1], column_r.at[d - 1],
                device(x, y, z + d, core),
            )
            for d in range(1, 8)
        ]
    )
    for c in across:
        c.wait()
    row_copies = row_copies + along_line(1, theirs)
    for c in row_copies:
        c.wait()
    picks = []
    for k in range(SLOTS):
        for h in range(2):
            for d in range(1, 4):
                wanted[k, h, d - 1] = group[h, asked[h, 3 - d, 2 * k + h, 0]]
                picks.append(
                    remote(
                        wanted.at[k, h, d - 1], chosen.at[k, h, d],
                        pick_s.at[k, h, d - 1], pick_r.at[k, h, d - 1], beside(1 - h, d),
                    )
                )
                picks[-1].start()
            chosen[k, h, 0] = group[h, places[k][h]]
    for c in columns:
        c.wait()
    total = piece[0]
    for d in range(7):
        total = total + column_in[d]
    piece[1] = total
    whole[me] = total

    def spread(e, _):
        to, _q = plane(e)
        remote(piece.at[1], whole.at[me], spread_s, spread_r, to).start()
        return 0

    lax.fori_loop(1, 32, spread, 0)
    for c in picks:
        c.wait()
    for k in range(SLOTS):
        for h in range(2):
            blocks[k, :, h * BLOCK : (h + 1) * BLOCK] = chosen[k, h, away[k][h]]
    for load in loads:
        load.wait()

    def contract(half, low):
        pieces = []
        for k in range(SLOTS):
            at = pl.multiple_of((half * HALF + low) * MONTHS, CHUNK * MONTHS)
            wide = jnp.dot(
                counts[k, pl.ds(at, CHUNK * MONTHS), :], blocks[k], preferred_element_type=F32
            )
            wide = wide.reshape(CHUNK, MONTHS, RANK) * month[...][None]
            pieces.append(jnp.sum(wide, axis=1) * live[k].astype(F32))
        for b in range(4):
            part[half, b, pl.ds(low, CHUNK), :] = add_three(
                [jnp.where(block_at[k] == b, pieces[k], 0.0) for k in range(SLOTS)]
            )

    def add_three(v):
        return v[0] + v[1] + v[2]

    pairs, line = [], []
    for which in range(2):
        half = 1 - core if which == 0 else core
        for n in range(HALF // CHUNK):
            at = pl.ds(n * CHUNK, CHUNK)
            contract(half, n * CHUNK)
            if which == 0:
                pairs.append(
                    remote(
                        part.at[half, :, at], pair_in.at[:, at], pair_s.at[n], pair_r.at[n],
                        device(x, y, z, 1 - core),
                    )
                )
                pairs[-1].start()
            else:
                pairs[n].wait()
                line_out[:, at] = part[half, :, at] + pair_in[:, at]
                for d in range(1, 4):
                    zt = lax.rem(zl + d, 4)
                    line.append(
                        remote(
                            line_out.at[zt, at], line_in.at[d - 1, at],
                            line_s.at[n, d - 1], line_r.at[n, d - 1], device(x, y, zh * 4 + zt, core),
                        )
                    )
                    line[-1].start()
    arrived(whole.at[0:31], spread_r)
    gram[...] = whole[...].reshape(RANK, RANK) * month_gram[...]
    first = gram[0:SIDE, :]
    _, before, after = eliminate(
        gram, 0, RANK // SIDE, (first, jnp.zeros_like(first), first)
    )
    clear_and_subtract(gram, RANK // SIDE - 1, before, after)
    for c in line:
        c.wait()
    share = line_out[zl] + line_in[0] + line_in[1] + line_in[2]
    out[...] = -jnp.dot(share, gram[...], precision=HI, preferred_element_type=F32)
    arrived(gram_own.at[0:31], plane_s)
    arrived(gram_own.at[0:31], spread_s)


def local(tiles, patient_block, owner, sub_block, live, code_factor, month_factor):
    dma, vmem = pltpu.SemaphoreType.DMA, pltpu.VMEM
    smem_spec = pl.BlockSpec(memory_space=pltpu.SMEM)
    vmem_spec = pl.BlockSpec(memory_space=pltpu.VMEM)
    return pl.pallas_call(
        kernel,
        out_shape=jax.ShapeDtypeStruct((HALF, RANK), F32),
        in_specs=[smem_spec] * 4 + [pl.BlockSpec(memory_space=pl.ANY)] * 3,
        out_specs=vmem_spec,
        scratch_shapes=[
            vmem((SLOTS, BLOCK * MONTHS, BLOCK), jnp.bfloat16),
            vmem((2 * BLOCK, RANK), jnp.bfloat16),
            vmem((MONTHS, RANK), F32),
            vmem((2, 16, BLOCK, BLOCK), jnp.bfloat16),
            vmem((8, 128), jnp.int32),
            vmem((2, 3, 8, 128), jnp.int32),
            pltpu.SMEM((2, 3, 8, 128), jnp.int32),
            vmem((SLOTS, 2, 3, BLOCK, BLOCK), jnp.bfloat16),
            vmem((SLOTS, 2, 4, BLOCK, BLOCK), jnp.bfloat16),
            vmem((SLOTS, BLOCK, RANK), jnp.bfloat16),
            vmem((32, 8, RANK), F32),
            vmem((31, 8, RANK), F32),
            vmem((2, 8, RANK), F32),
            vmem((7, 8, RANK), F32),
            vmem((32, 8, RANK), F32),
            vmem((RANK, RANK), F32),
            vmem((RANK, RANK), F32),
            vmem((2, 4, HALF, RANK), F32),
            vmem((4, HALF, RANK), F32),
            vmem((4, HALF, RANK), F32),
            vmem((3, HALF, RANK), F32),
            dma((SLOTS,)),
            dma((2,)),
            dma((2, 3)),
            dma((2, 3)),
            dma,
            dma((2,)),
            dma((2,)),
            dma((2, 2, 3)),
            dma((2, 2, 3)),
            dma((SLOTS, 2, 3)),
            dma((SLOTS, 2, 3)),
            dma,
            dma,
            dma((7,)),
            dma((7,)),
            dma,
            dma,
            dma((HALF // CHUNK,)),
            dma((HALF // CHUNK,)),
            dma((HALF // CHUNK, 3)),
            dma((HALF // CHUNK, 3)),
        ],
        compiler_params=pltpu.CompilerParams(
            collective_id=0, has_side_effects=True, vmem_limit_bytes=56 << 20
        ),
        cost_estimate=pl.CostEstimate(
            flops=3_300_000_000, bytes_accessed=12_000_000, transcendentals=0
        ),
    )(
        owner.reshape(SLOTS),
        sub_block,
        patient_block,
        live,
        tiles.reshape(SLOTS, BLOCK * MONTHS, BLOCK),
        code_factor,
        month_factor,
    )


def solution(mesh):
    placed = (
        P(("pat", "code"), None, None, None),
        P(("pat", "code")),
        P(("pat", "code"), None),
        P(("pat", "code")),
        P(("pat", "code")),
        P(("pat", "code"), None),
        P(),
    )
    return jax.shard_map(
        local, mesh=mesh, in_specs=placed, out_specs=P(("pat", "code"), None), check_vma=False
    )
```

```python
import jax
import jax.numpy as jnp
from jax import lax
from jax.experimental import pallas as pl
from jax.experimental.pallas import tpu as pltpu
from jax.sharding import PartitionSpec as P

MESH = pl.DeviceIdType.MESH
HI = lax.Precision.HIGHEST
F32 = jnp.float32
BLOCK = 128
MONTHS = 120
RANK = 256
SLOTS = 3
HALF = 64
CHUNK = 32
SIDE = 32


def recip(p):
    r = pltpu.reciprocal(p, approx=True)
    return r * (2.0 - p * r)


def tree(values, bits):
    while len(values) > 1:
        values = [
            jnp.where(bits[0], values[i + 1], values[i]) for i in range(0, len(values), 2)
        ]
        bits = bits[1:]
    return values[0]


def add_up(values):
    while len(values) > 1:
        values = [values[i] + values[i + 1] for i in range(0, len(values), 2)]
    return values[0]


def lane_of(v, at):
    return jnp.broadcast_to(v[:, at : at + 1], (8, 128))


def row_of(v, at):
    return jnp.broadcast_to(v[at : at + 1, :], (8, 128))


def sweep_pairs(d):
    n = 8

    def at(i, j):
        return d[min(i, j), max(i, j)]

    for k in range(0, n, 2):
        a, b, c = at(k, k), at(k, k + 1), at(k + 1, k + 1)
        r = recip(a * c - b * b)
        ia, ib, ic = c * r, b * r, a * r
        rest = [i for i in range(n) if i > k + 1] + [i for i in range(n) if i < k]
        u = {
            i: (ia * at(k, i) - ib * at(k + 1, i), ic * at(k + 1, i) - ib * at(k, i)) for i in rest
        }
        new = {}
        for p, i in enumerate(rest):
            for j in rest[p:]:
                new[min(i, j), max(i, j)] = at(i, j) - (at(k, i) * u[j][0] + at(k + 1, i) * u[j][1])
        for i in rest:
            new[min(i, k), max(i, k)] = u[i][0]
            new[min(i, k + 1), max(i, k + 1)] = u[i][1]
        new[k, k], new[k, k + 1], new[k + 1, k + 1] = -ia, ib, -ic
        d = new
    return d


def panel(rows, half, l0, row, lane):
    c = [lane_of(rows[half], l0 + m) for m in range(8)]
    lines = [[row_of(rows[h], m) for m in range(8)] for h in range(2)]
    d = sweep_pairs({(i, j): row_of(c[j], i) for i in range(8) for j in range(i, 8)})
    row_bits = [(row & b) == b for b in (1, 2, 4)]
    rel = lane - l0
    lane_bits = [(rel & b) == b for b in (1, 2, 4)]
    minus = [tree([d[min(i, m), max(i, m)] for i in range(8)], row_bits) for m in range(8)]
    inside = -tree(minus, lane_bits)
    out = []
    for h in range(2):
        w = -add_up([minus[m] * lines[h][m] for m in range(8)])
        out.append(jnp.where((rel >= 0) & (rel < 8), inside, w) if h == half else w)
    return out


def turned_dot(a, b):
    return lax.dot_general(
        a, b, (((0,), (0,)), ((), ())), precision=HI, preferred_element_type=F32
    )


def clear_and_subtract(a, s, rows, done):
    wide = lax.broadcasted_iota(jnp.int32, (1, RANK), 1)
    o = s * SIDE
    inside = (wide >= o) & (wide < o + SIDE)
    a[...] = jnp.where(inside, 0.0, a[...]) - turned_dot(rows, done)
    a[pl.ds(pl.multiple_of(jnp.maximum(o, 0), SIDE), SIDE), :] = done


def eliminate(a, first, last, carry, beside=None, after_step=None):
    row = lax.broadcasted_iota(jnp.int32, (8, 128), 0)
    lane = lax.broadcasted_iota(jnp.int32, (8, 128), 1)
    wide = lax.broadcasted_iota(jnp.int32, (1, RANK), 1)
    n = SIDE // 8

    def step(s, carry):
        turned, before, after = carry
        clear_and_subtract(a, s - 1, before, after)
        o = pl.multiple_of(s * SIDE, SIDE)
        ahead = pl.multiple_of(lax.rem(o + SIDE, RANK), SIDE)
        following = pltpu.roll(a[pl.ds(ahead, SIDE), :], RANK - o, 1)
        straight = pltpu.roll(turned, o, 1)
        rows = [[turned[8 * j : 8 * j + 8, :128], turned[8 * j : 8 * j + 8, 128:]] for j in range(n)]
        for j in range(n):
            l0 = 8 * j
            order = list(range(j + 1, n)) + list(range(j))
            factor = {i: [lane_of(rows[i][0], l0 + m) for m in range(8)] for i in order}
            if beside is not None and j == 1:
                beside(s)
            rows[j] = panel(rows[j], 0, l0, row, lane)
            inside = (lane >= l0) & (lane < l0 + 8)
            w = [[row_of(rows[j][h], m) for m in range(8)] for h in range(2)]
            for i in order:
                for h in range(2):
                    old = jnp.where(inside, 0.0, rows[i][h]) if h == 0 else rows[i][h]
                    rows[i][h] = old - add_up([factor[i][m] * w[h][m] for m in range(8)])
        done = jnp.concatenate([jnp.concatenate(r, axis=1) for r in rows], axis=0)
        done = jnp.where(wide < SIDE, -done, done)
        following = jnp.where(wide < SIDE, 0.0, following) - turned_dot(
            turned[:, SIDE : 2 * SIDE], done
        )
        result = pltpu.roll(following, RANK - SIDE, 1), straight, pltpu.roll(done, o, 1)
        if after_step is not None:
            after_step(s)
        return result

    return lax.fori_loop(first, last, step, carry)


def kernel(
    owner, sub, block_at, live, tiles, code_in, month_in, out,
    counts, code, month, group, need, need_in, asked, wanted, chosen, blocks,
    gram_own, plane_in, piece, column_in, whole, gram, month_gram,
    part, pair_in, line_out, line_in,
    tile_sem, small_sem, need_s, need_r, asked_sem, zh_s, zh_r, row_s, row_r, pick_s, pick_r,
    plane_s, plane_r, column_s, column_r, spread_s, spread_r, halves_s, halves_r,
    pair_s, pair_r, line_s, line_r,
):
    pat, code_at = lax.axis_index("pat"), lax.axis_index("code")
    x, y, zh = pat // 8, (pat // 2) % 4, pat % 2
    zl, core = code_at // 2, code_at % 2
    z = zh * 4 + zl
    spot = x * 4 + y
    me = core * 16 + spot

    def device(x, y, z, c):
        x, y, z = lax.rem(x, 4), lax.rem(y, 4), lax.rem(z, 8)
        return ((x * 4 + y) * 2 + z // 4, lax.rem(z, 4) * 2 + c)

    def plane(e):
        px, py, pc = lax.rem(x + e // 8, 4), lax.rem(y + (e // 2) % 4, 4), lax.rem(core + e % 2, 2)
        return device(px, py, z, pc), pc * 16 + px * 4 + py

    def beside(h, d):
        return device(x + d, y, z, core) if h == 0 else device(x, y + d, z, core)

    def remote(src, dst, send, recv, to):
        return pltpu.make_async_remote_copy(
            src_ref=src, dst_ref=dst, send_sem=send, recv_sem=recv, device_id=to, device_id_type=MESH
        )

    def start(copies):
        for c in copies:
            c.start()
        return copies

    def arrived(buf, sem):
        pltpu.make_async_copy(buf, buf, sem).wait()

    small = start(
        [
            pltpu.make_async_copy(code_in, code, small_sem.at[0]),
            pltpu.make_async_copy(month_in, month, small_sem.at[1]),
        ]
    )
    loads = start(
        [pltpu.make_async_copy(tiles.at[k], counts.at[k], tile_sem.at[k]) for k in range(SLOTS)]
    )
    barrier = pltpu.get_barrier_semaphore()

    def greet(e, _):
        pl.semaphore_signal(barrier, inc=1, device_id=plane(e)[0], device_id_type=MESH)
        return 0

    for d in (4, 3, 5, 2, 6, 1, 7):
        pl.semaphore_signal(
            barrier, inc=1, device_id=device(x, y, z + d, core), device_id_type=MESH
        )
    lax.fori_loop(1, 32, greet, 0)
    line_at = lax.broadcasted_iota(jnp.int32, (8, 128), 0)
    places, away = [], []
    for k in range(SLOTS):
        o = owner[k]
        ox, oy, oz = o // 8, (o // 2) % 4, o % 2
        places.append([(oz * 4 + ox) * 2 + sub[k], (oz * 4 + oy) * 2 + sub[k]])
        away.append([lax.rem(y + 4 - oy, 4), lax.rem(x + 4 - ox, 4)])
    wish = jnp.zeros((8, 128), jnp.int32)
    for k in range(SLOTS):
        for h in range(2):
            wish = jnp.where(line_at == 2 * k + h, places[k][h], wish)
    need[...] = wish
    mine = [(zh * 4 + x) * 2, (zh * 4 + y) * 2]
    theirs = [((1 - zh) * 4 + x) * 2, ((1 - zh) * 4 + y) * 2]
    small[0].wait()
    for h in range(2):
        for b in range(2):
            group[h, mine[h] + b] = code[b * BLOCK : (b + 1) * BLOCK, h * BLOCK : (h + 1) * BLOCK]
    pl.semaphore_wait(barrier, 38)

    across = []
    for b in range(2):
        for h in range(2):
            here = group.at[h, mine[h] + b]
            across.append(remote(here, here, zh_s.at[b, h], zh_r.at[b, h], device(x, y, z + 4, core)))
    start(across)
    needs = start(
        [
            remote(need, need_in.at[h, d - 1], need_s.at[h, d - 1], need_r.at[h, d - 1], beside(1 - h, d))
            for h in range(2)
            for d in range(1, 4)
        ]
    )

    own = lax.dot_general(
        code[...], code[...], (((0,), (0,)), ((), ())), preferred_element_type=F32
    )
    gram_own[...] = own.reshape(32, 8, RANK)

    def scatter(e, _):
        to, q = plane(e)
        remote(gram_own.at[q], plane_in.at[e - 1], plane_s, plane_r, to).start()
        return 0

    lax.fori_loop(1, 32, scatter, 0)

    def along_line(s, first, count):
        copies = []
        for h in range(2):
            here = group.at[h, pl.ds(first[h], count)]
            for d in range(1, 4):
                copies.append(
                    remote(here, here, row_s.at[s, h, d - 1], row_r.at[s, h, d - 1], beside(h, d))
                )
        return start(copies)

    row_copies = along_line(0, mine, 2)
    small[1].wait()
    month_gram[...] = turned_dot(month[...], month[...])
    for c in needs:
        c.wait()
    to_scalars = pltpu.make_async_copy(need_in, asked, asked_sem)
    to_scalars.start()
    to_scalars.wait()
    for c in across[:2]:
        c.wait()
    row_copies = row_copies + along_line(1, theirs, 1)
    arrived(plane_in, plane_r)
    piece[0] = lax.fori_loop(0, 31, lambda e, t: t + plane_in[e], gram_own[me], unroll=True)
    columns = start(
        [
            remote(
                piece.at[0], column_in.at[d - 1], column_s.at[d - 1], column_r.at[d - 1],
                device(x, y, z + d, core),
            )
            for d in range(1, 8)
        ]
    )
    for c in across[2:]:
        c.wait()
    row_copies = row_copies + along_line(2, [t + 1 for t in theirs], 1)
    for c in columns:
        c.wait()
    total = piece[0]
    for d in range(7):
        total = total + column_in[d]
    piece[1] = total
    whole[core, spot] = total

    def spread(e, _):
        to = device(x + e // 4, y + e % 4, z, core)
        remote(piece.at[1], whole.at[core, spot], spread_s, spread_r, to).start()
        return 0

    lax.fori_loop(1, 16, spread, 0)
    for c in row_copies:
        c.wait()
    picks = []
    for k in range(SLOTS):
        for h in range(2):
            for d in range(1, 4):
                wanted[k, h, d - 1] = group[h, asked[h, 3 - d, 2 * k + h, 0]]
                picks.append(
                    remote(
                        wanted.at[k, h, d - 1], chosen.at[k, h, d],
                        pick_s.at[k, h, d - 1], pick_r.at[k, h, d - 1], beside(1 - h, d),
                    )
                )
                picks[-1].start()
            chosen[k, h, 0] = group[h, places[k][h]]
    arrived(whole.at[0, 0:15], spread_r)
    halves = remote(
        whole.at[core], whole.at[core], halves_s, halves_r, device(x, y, z, 1 - core)
    )
    halves.start()
    halves.wait()
    gram[...] = whole[...].reshape(RANK, RANK) * month_gram[...]
    first = gram[0:SIDE, :]
    for c in picks:
        c.wait()
    for k in range(SLOTS):
        for h in range(2):
            blocks[k, :, h * BLOCK : (h + 1) * BLOCK] = chosen[k, h, away[k][h]]
    for load in loads:
        load.wait()

    per_half = HALF // CHUNK

    def contract(s):
        half = jnp.where(s < per_half, 1 - core, core)
        low = pl.multiple_of(lax.rem(s, per_half) * CHUNK, CHUNK)
        at = pl.multiple_of((half * HALF + low) * MONTHS, CHUNK * MONTHS)
        pieces = []
        for k in range(SLOTS):
            wide = jnp.dot(
                counts[k, pl.ds(at, CHUNK * MONTHS), :], blocks[k], preferred_element_type=F32
            )
            wide = wide.reshape(CHUNK, MONTHS, RANK) * month[...][None]
            pieces.append(jnp.sum(wide, axis=1) * live[k].astype(F32))
        for b in range(4):
            chosen_pieces = [jnp.where(block_at[k] == b, pieces[k], 0.0) for k in range(SLOTS)]
            part[half, b, pl.ds(low, CHUNK), :] = chosen_pieces[0] + chosen_pieces[1] + chosen_pieces[2]

    def pair_copy(n):
        at = pl.ds(pl.multiple_of(n * CHUNK, CHUNK), CHUNK)
        return remote(
            part.at[1 - core, :, at], pair_in.at[:, at], pair_s.at[n], pair_r.at[n],
            device(x, y, z, 1 - core),
        )

    def line_copy(n, d):
        at = pl.ds(pl.multiple_of(n * CHUNK, CHUNK), CHUNK)
        zt = lax.rem(zl + d, 4)
        return remote(
            line_out.at[zt, at], line_in.at[d - 1, at], line_s.at[n, d - 1], line_r.at[n, d - 1],
            device(x, y, zh * 4 + zt, core),
        )

    def send_sums(s):
        @pl.when(s < per_half)
        def _():
            pair_copy(s).start()

        @pl.when(s >= per_half)
        def _():
            n = s - per_half
            at = pl.ds(pl.multiple_of(n * CHUNK, CHUNK), CHUNK)
            pair_copy(n).wait()
            line_out[:, at] = part[core, :, at] + pair_in[:, at]
            for d in range(1, 4):
                line_copy(n, d).start()

    carry = (first, jnp.zeros_like(first), first)
    carry = eliminate(gram, 0, 2 * per_half, carry, contract, send_sums)
    line = [line_copy(n, d) for n in range(per_half) for d in range(1, 4)]
    _, before, after = eliminate(gram, 2 * per_half, RANK // SIDE, carry)
    clear_and_subtract(gram, RANK // SIDE - 1, before, after)
    for c in line:
        c.wait()
    share = line_out[zl] + line_in[0] + line_in[1] + line_in[2]
    out[...] = -jnp.dot(share, gram[...], precision=HI, preferred_element_type=F32)
    arrived(gram_own.at[0:31], plane_s)
    arrived(gram_own.at[0:15], spread_s)


def local(tiles, patient_block, owner, sub_block, live, code_factor, month_factor):
    dma, vmem = pltpu.SemaphoreType.DMA, pltpu.VMEM
    smem_spec = pl.BlockSpec(memory_space=pltpu.SMEM)
    vmem_spec = pl.BlockSpec(memory_space=pltpu.VMEM)
    return pl.pallas_call(
        kernel,
        out_shape=jax.ShapeDtypeStruct((HALF, RANK), F32),
        in_specs=[smem_spec] * 4 + [pl.BlockSpec(memory_space=pl.ANY)] * 3,
        out_specs=vmem_spec,
        scratch_shapes=[
            vmem((SLOTS, BLOCK * MONTHS, BLOCK), jnp.bfloat16),
            vmem((2 * BLOCK, RANK), jnp.bfloat16),
            vmem((MONTHS, RANK), F32),
            vmem((2, 16, BLOCK, BLOCK), jnp.bfloat16),
            vmem((8, 128), jnp.int32),
            vmem((2, 3, 8, 128), jnp.int32),
            pltpu.SMEM((2, 3, 8, 128), jnp.int32),
            vmem((SLOTS, 2, 3, BLOCK, BLOCK), jnp.bfloat16),
            vmem((SLOTS, 2, 4, BLOCK, BLOCK), jnp.bfloat16),
            vmem((SLOTS, BLOCK, RANK), jnp.bfloat16),
            vmem((32, 8, RANK), F32),
            vmem((31, 8, RANK), F32),
            vmem((2, 8, RANK), F32),
            vmem((7, 8, RANK), F32),
            vmem((2, 16, 8, RANK), F32),
            vmem((RANK, RANK), F32),
            vmem((RANK, RANK), F32),
            vmem((2, 4, HALF, RANK), F32),
            vmem((4, HALF, RANK), F32),
            vmem((4, HALF, RANK), F32),
            vmem((3, HALF, RANK), F32),
            dma((SLOTS,)),
            dma((2,)),
            dma((2, 3)),
            dma((2, 3)),
            dma,
            dma((2, 2)),
            dma((2, 2)),
            dma((3, 2, 3)),
            dma((3, 2, 3)),
            dma((SLOTS, 2, 3)),
            dma((SLOTS, 2, 3)),
            dma,
            dma,
            dma((7,)),
            dma((7,)),
            dma,
            dma,
            dma,
            dma,
            dma((HALF // CHUNK,)),
            dma((HALF // CHUNK,)),
            dma((HALF // CHUNK, 3)),
            dma((HALF // CHUNK, 3)),
        ],
        compiler_params=pltpu.CompilerParams(
            collective_id=0, has_side_effects=True, vmem_limit_bytes=56 << 20
        ),
        cost_estimate=pl.CostEstimate(
            flops=3_300_000_000, bytes_accessed=12_000_000, transcendentals=0
        ),
    )(
        owner.reshape(SLOTS),
        sub_block,
        patient_block,
        live,
        tiles.reshape(SLOTS, BLOCK * MONTHS, BLOCK),
        code_factor,
        month_factor,
    )


def solution(mesh):
    placed = (
        P(("pat", "code"), None, None, None),
        P(("pat", "code")),
        P(("pat", "code"), None),
        P(("pat", "code")),
        P(("pat", "code")),
        P(("pat", "code"), None),
        P(),
    )
    return jax.shard_map(
        local, mesh=mesh, in_specs=placed, out_specs=P(("pat", "code"), None), check_vma=False
    )
```

```python
import jax
import jax.numpy as jnp
from jax import lax
from jax.experimental import pallas as pl
from jax.experimental.pallas import tpu as pltpu
from jax.sharding import PartitionSpec as P

MESH = pl.DeviceIdType.MESH
HI = lax.Precision.HIGHEST
F32 = jnp.float32
BLOCK = 128
MONTHS = 120
RANK = 256
SLOTS = 3
HALF = 64
CHUNK = 32
SIDE = 32


def recip(p):
    r = pltpu.reciprocal(p, approx=True)
    return r * (2.0 - p * r)


def tree(values, bits):
    while len(values) > 1:
        values = [
            jnp.where(bits[0], values[i + 1], values[i]) for i in range(0, len(values), 2)
        ]
        bits = bits[1:]
    return values[0]


def add_up(values):
    while len(values) > 1:
        values = [values[i] + values[i + 1] for i in range(0, len(values), 2)]
    return values[0]


def lane_of(v, at):
    return jnp.broadcast_to(v[:, at : at + 1], (8, 128))


def row_of(v, at):
    return jnp.broadcast_to(v[at : at + 1, :], (8, 128))


def sweep_pairs(d):
    n = 8

    def at(i, j):
        return d[min(i, j), max(i, j)]

    for k in range(0, n, 2):
        a, b, c = at(k, k), at(k, k + 1), at(k + 1, k + 1)
        r = recip(a * c - b * b)
        ia, ib, ic = c * r, b * r, a * r
        rest = [i for i in range(n) if i > k + 1] + [i for i in range(n) if i < k]
        u = {
            i: (ia * at(k, i) - ib * at(k + 1, i), ic * at(k + 1, i) - ib * at(k, i)) for i in rest
        }
        new = {}
        for p, i in enumerate(rest):
            for j in rest[p:]:
                new[min(i, j), max(i, j)] = at(i, j) - (at(k, i) * u[j][0] + at(k + 1, i) * u[j][1])
        for i in rest:
            new[min(i, k), max(i, k)] = u[i][0]
            new[min(i, k + 1), max(i, k + 1)] = u[i][1]
        new[k, k], new[k, k + 1], new[k + 1, k + 1] = -ia, ib, -ic
        d = new
    return d


def panel(rows, half, l0, row, lane):
    c = [lane_of(rows[half], l0 + m) for m in range(8)]
    lines = [[row_of(rows[h], m) for m in range(8)] for h in range(2)]
    d = sweep_pairs({(i, j): row_of(c[j], i) for i in range(8) for j in range(i, 8)})
    row_bits = [(row & b) == b for b in (1, 2, 4)]
    rel = lane - l0
    lane_bits = [(rel & b) == b for b in (1, 2, 4)]
    minus = [tree([d[min(i, m), max(i, m)] for i in range(8)], row_bits) for m in range(8)]
    inside = -tree(minus, lane_bits)
    out = []
    for h in range(2):
        w = -add_up([minus[m] * lines[h][m] for m in range(8)])
        out.append(jnp.where((rel >= 0) & (rel < 8), inside, w) if h == half else w)
    return out


def turned_dot(a, b):
    return lax.dot_general(
        a, b, (((0,), (0,)), ((), ())), precision=HI, preferred_element_type=F32
    )


def clear_and_subtract(a, s, rows, done):
    wide = lax.broadcasted_iota(jnp.int32, (1, RANK), 1)
    o = s * SIDE
    inside = (wide >= o) & (wide < o + SIDE)
    a[...] = jnp.where(inside, 0.0, a[...]) - turned_dot(rows, done)
    a[pl.ds(pl.multiple_of(jnp.maximum(o, 0), SIDE), SIDE), :] = done


def eliminate(a, first, last, carry, beside=None, after_step=None):
    row = lax.broadcasted_iota(jnp.int32, (8, 128), 0)
    lane = lax.broadcasted_iota(jnp.int32, (8, 128), 1)
    wide = lax.broadcasted_iota(jnp.int32, (1, RANK), 1)
    n = SIDE // 8

    def step(s, carry):
        turned, before, after = carry
        clear_and_subtract(a, s - 1, before, after)
        o = pl.multiple_of(s * SIDE, SIDE)
        ahead = pl.multiple_of(lax.rem(o + SIDE, RANK), SIDE)
        following = pltpu.roll(a[pl.ds(ahead, SIDE), :], RANK - o, 1)
        straight = pltpu.roll(turned, o, 1)
        rows = [[turned[8 * j : 8 * j + 8, :128], turned[8 * j : 8 * j + 8, 128:]] for j in range(n)]
        for j in range(n):
            l0 = 8 * j
            order = list(range(j + 1, n)) + list(range(j))
            factor = {i: [lane_of(rows[i][0], l0 + m) for m in range(8)] for i in order}
            if beside is not None and j == 1:
                beside(s)
            rows[j] = panel(rows[j], 0, l0, row, lane)
            inside = (lane >= l0) & (lane < l0 + 8)
            w = [[row_of(rows[j][h], m) for m in range(8)] for h in range(2)]
            for i in order:
                for h in range(2):
                    old = jnp.where(inside, 0.0, rows[i][h]) if h == 0 else rows[i][h]
                    rows[i][h] = old - add_up([factor[i][m] * w[h][m] for m in range(8)])
        done = jnp.concatenate([jnp.concatenate(r, axis=1) for r in rows], axis=0)
        done = jnp.where(wide < SIDE, -done, done)
        following = jnp.where(wide < SIDE, 0.0, following) - turned_dot(
            turned[:, SIDE : 2 * SIDE], done
        )
        result = pltpu.roll(following, RANK - SIDE, 1), straight, pltpu.roll(done, o, 1)
        if after_step is not None:
            after_step(s)
        return result

    return lax.fori_loop(first, last, step, carry)


def far_first(offsets, hops):
    return sorted(offsets, key=hops, reverse=True)


RING = (0, 1, 2, 1)
PLANE = far_first(range(1, 32), lambda e: RING[e // 8] + RING[e // 2 % 4])
SPOTS = far_first(range(1, 16), lambda e: RING[e // 4] + RING[e % 4])
COLUMN = far_first(range(1, 8), lambda d: min(d, 8 - d))
LINE = (2, 1, 3)


def kernel(
    owner_in, sub_in, block_in, live_in, tiles, code_in, month_in, out, owner, sub, block_at, live,
    counts, code, month, group, need, need_in, asked, wanted, chosen, blocks,
    gram_own, plane_in, piece, column_in, whole, gram, month_gram,
    part, pair_in, line_out, line_in,
    scalar_sem, tile_sem, small_sem, need_s, need_r, asked_sem, zh_s, zh_r, row_s, row_r, pick_s, pick_r,
    plane_s, plane_r, column_s, column_r, spread_s, spread_r, halves_s, halves_r,
    pair_s, pair_r, line_s, line_r,
):
    pat, code_at = lax.axis_index("pat"), lax.axis_index("code")
    x, y, zh = pat // 8, (pat // 2) % 4, pat % 2
    zl, core = code_at // 2, code_at % 2
    z = zh * 4 + zl
    spot = x * 4 + y
    me = core * 16 + spot

    def device(x, y, z, c):
        x, y, z = lax.rem(x, 4), lax.rem(y, 4), lax.rem(z, 8)
        return ((x * 4 + y) * 2 + z // 4, lax.rem(z, 4) * 2 + c)

    def plane(e):
        px, py, pc = lax.rem(x + e // 8, 4), lax.rem(y + (e // 2) % 4, 4), core
        if e % 2:
            pc = 1 - core
        return device(px, py, z, pc), pc * 16 + px * 4 + py

    def beside(h, d):
        return device(x + d, y, z, core) if h == 0 else device(x, y + d, z, core)

    def remote(src, dst, send, recv, to):
        return pltpu.make_async_remote_copy(
            src_ref=src, dst_ref=dst, send_sem=send, recv_sem=recv, device_id=to, device_id_type=MESH
        )

    def start(copies):
        for c in copies:
            c.start()
        return copies

    def arrived(buf, sem):
        pltpu.make_async_copy(buf, buf, sem).wait()

    small = start(
        [
            pltpu.make_async_copy(code_in, code, small_sem.at[0]),
            pltpu.make_async_copy(month_in, month, small_sem.at[1]),
        ]
    )
    loads = start(
        [pltpu.make_async_copy(tiles.at[k], counts.at[k], tile_sem.at[k]) for k in range(SLOTS)]
    )
    scalars = start(
        [
            pltpu.make_async_copy(src, dst, scalar_sem.at[n])
            for n, (src, dst) in enumerate(
                ((owner_in, owner), (sub_in, sub), (block_in, block_at), (live_in, live))
            )
        ]
    )
    barrier = pltpu.get_barrier_semaphore()

    for d in COLUMN:
        pl.semaphore_signal(
            barrier, inc=1, device_id=device(x, y, z + d, core), device_id_type=MESH
        )
    for e in PLANE:
        pl.semaphore_signal(barrier, inc=1, device_id=plane(e)[0], device_id_type=MESH)
    for c in scalars:
        c.wait()
    line_at = lax.broadcasted_iota(jnp.int32, (8, 128), 0)
    places, away = [], []
    for k in range(SLOTS):
        o = owner[k]
        ox, oy, oz = o // 8, (o // 2) % 4, o % 2
        places.append([(oz * 4 + ox) * 2 + sub[k], (oz * 4 + oy) * 2 + sub[k]])
        away.append([lax.rem(y + 4 - oy, 4), lax.rem(x + 4 - ox, 4)])
    wish = jnp.zeros((8, 128), jnp.int32)
    for k in range(SLOTS):
        for h in range(2):
            wish = jnp.where(line_at == 2 * k + h, places[k][h], wish)
    need[...] = wish
    mine = [(zh * 4 + x) * 2, (zh * 4 + y) * 2]
    theirs = [((1 - zh) * 4 + x) * 2, ((1 - zh) * 4 + y) * 2]
    small[0].wait()
    for h in range(2):
        for b in range(2):
            group[h, mine[h] + b] = code[b * BLOCK : (b + 1) * BLOCK, h * BLOCK : (h + 1) * BLOCK]
    pl.semaphore_wait(barrier, 38)

    across = []
    for b in range(2):
        for h in range(2):
            here = group.at[h, mine[h] + b]
            across.append(remote(here, here, zh_s.at[b, h], zh_r.at[b, h], device(x, y, z + 4, core)))
    start(across)
    needs = start(
        [
            remote(need, need_in.at[h, d - 1], need_s.at[h, d - 1], need_r.at[h, d - 1], beside(1 - h, d))
            for h in range(2)
            for d in range(1, 4)
        ]
    )

    own = lax.dot_general(
        code[...], code[...], (((0,), (0,)), ((), ())), preferred_element_type=F32
    )
    gram_own[...] = own.reshape(32, 8, RANK)

    for e in PLANE:
        to, q = plane(e)
        remote(gram_own.at[q], plane_in.at[e - 1], plane_s, plane_r, to).start()

    def along_line(s, first, count):
        copies = []
        for h in range(2):
            here = group.at[h, pl.ds(first[h], count)]
            for d in LINE:
                copies.append(
                    remote(here, here, row_s.at[s, h, d - 1], row_r.at[s, h, d - 1], beside(h, d))
                )
        return start(copies)

    row_copies = along_line(0, mine, 2)
    small[1].wait()
    month_gram[...] = turned_dot(month[...], month[...])
    for c in needs:
        c.wait()
    to_scalars = pltpu.make_async_copy(need_in, asked, asked_sem)
    to_scalars.start()
    to_scalars.wait()
    for c in across[:2]:
        c.wait()
    row_copies = row_copies + along_line(1, theirs, 1)
    arrived(plane_in, plane_r)
    piece[0] = lax.fori_loop(0, 31, lambda e, t: t + plane_in[e], gram_own[me], unroll=True)
    columns = start(
        [
            remote(
                piece.at[0], column_in.at[d - 1], column_s.at[d - 1], column_r.at[d - 1],
                device(x, y, z + d, core),
            )
            for d in COLUMN
        ]
    )
    for c in across[2:]:
        c.wait()
    row_copies = row_copies + along_line(2, [t + 1 for t in theirs], 1)
    for c in columns:
        c.wait()
    total = piece[0]
    for d in range(7):
        total = total + column_in[d]
    piece[1] = total
    whole[core, spot] = total

    for e in SPOTS:
        to = device(x + e // 4, y + e % 4, z, core)
        remote(piece.at[1], whole.at[core, spot], spread_s, spread_r, to).start()
    for c in row_copies:
        c.wait()
    picks = []
    for k in range(SLOTS):
        for h in range(2):
            for d in LINE:
                wanted[k, h, d - 1] = group[h, asked[h, 3 - d, 2 * k + h, 0]]
                picks.append(
                    remote(
                        wanted.at[k, h, d - 1], chosen.at[k, h, d],
                        pick_s.at[k, h, d - 1], pick_r.at[k, h, d - 1], beside(1 - h, d),
                    )
                )
                picks[-1].start()
            chosen[k, h, 0] = group[h, places[k][h]]
    arrived(whole.at[0, 0:15], spread_r)
    halves = remote(
        whole.at[core], whole.at[core], halves_s, halves_r, device(x, y, z, 1 - core)
    )
    halves.start()
    halves.wait()
    gram[...] = whole[...].reshape(RANK, RANK) * month_gram[...]
    first = gram[0:SIDE, :]
    for c in picks:
        c.wait()
    for k in range(SLOTS):
        for h in range(2):
            blocks[k, :, h * BLOCK : (h + 1) * BLOCK] = chosen[k, h, away[k][h]]
    for load in loads:
        load.wait()

    per_half = HALF // CHUNK

    def contract(s):
        half = jnp.where(s < per_half, 1 - core, core)
        low = pl.multiple_of(lax.rem(s, per_half) * CHUNK, CHUNK)
        at = pl.multiple_of((half * HALF + low) * MONTHS, CHUNK * MONTHS)
        pieces = []
        for k in range(SLOTS):
            wide = jnp.dot(
                counts[k, pl.ds(at, CHUNK * MONTHS), :], blocks[k], preferred_element_type=F32
            )
            wide = wide.reshape(CHUNK, MONTHS, RANK) * month[...][None]
            pieces.append(jnp.sum(wide, axis=1) * live[k].astype(F32))
        for b in range(4):
            chosen_pieces = [jnp.where(block_at[k] == b, pieces[k], 0.0) for k in range(SLOTS)]
            part[half, b, pl.ds(low, CHUNK), :] = chosen_pieces[0] + chosen_pieces[1] + chosen_pieces[2]

    def pair_copy(n):
        at = pl.ds(pl.multiple_of(n * CHUNK, CHUNK), CHUNK)
        return remote(
            part.at[1 - core, :, at], pair_in.at[:, at], pair_s.at[n], pair_r.at[n],
            device(x, y, z, 1 - core),
        )

    def line_copy(n, d):
        at = pl.ds(pl.multiple_of(n * CHUNK, CHUNK), CHUNK)
        zt = lax.rem(zl + d, 4)
        return remote(
            line_out.at[zt, at], line_in.at[d - 1, at], line_s.at[n, d - 1], line_r.at[n, d - 1],
            device(x, y, zh * 4 + zt, core),
        )

    def send_sums(s):
        @pl.when(s < per_half)
        def _():
            pair_copy(s).start()

        @pl.when(s >= per_half)
        def _():
            n = s - per_half
            at = pl.ds(pl.multiple_of(n * CHUNK, CHUNK), CHUNK)
            pair_copy(n).wait()
            line_out[:, at] = part[core, :, at] + pair_in[:, at]
            for d in range(1, 4):
                line_copy(n, d).start()

    carry = (first, jnp.zeros_like(first), first)
    carry = eliminate(gram, 0, 2 * per_half, carry, contract, send_sums)
    line = [line_copy(n, d) for n in range(per_half) for d in range(1, 4)]
    _, before, after = eliminate(gram, 2 * per_half, RANK // SIDE, carry)
    clear_and_subtract(gram, RANK // SIDE - 1, before, after)
    for c in line:
        c.wait()
    share = line_out[zl] + line_in[0] + line_in[1] + line_in[2]
    out[...] = -jnp.dot(share, gram[...], precision=HI, preferred_element_type=F32)
    arrived(gram_own.at[0:31], plane_s)
    arrived(gram_own.at[0:15], spread_s)


def local(tiles, patient_block, owner, sub_block, live, code_factor, month_factor):
    dma, vmem = pltpu.SemaphoreType.DMA, pltpu.VMEM
    vmem_spec = pl.BlockSpec(memory_space=pltpu.VMEM)
    return pl.pallas_call(
        kernel,
        out_shape=jax.ShapeDtypeStruct((HALF, RANK), F32),
        in_specs=[pl.BlockSpec(memory_space=pl.ANY)] * 7,
        out_specs=vmem_spec,
        scratch_shapes=[
            *[pltpu.SMEM((SLOTS,), jnp.int32)] * 4,
            vmem((SLOTS, BLOCK * MONTHS, BLOCK), jnp.bfloat16),
            vmem((2 * BLOCK, RANK), jnp.bfloat16),
            vmem((MONTHS, RANK), F32),
            vmem((2, 16, BLOCK, BLOCK), jnp.bfloat16),
            vmem((8, 128), jnp.int32),
            vmem((2, 3, 8, 128), jnp.int32),
            pltpu.SMEM((2, 3, 8, 128), jnp.int32),
            vmem((SLOTS, 2, 3, BLOCK, BLOCK), jnp.bfloat16),
            vmem((SLOTS, 2, 4, BLOCK, BLOCK), jnp.bfloat16),
            vmem((SLOTS, BLOCK, RANK), jnp.bfloat16),
            vmem((32, 8, RANK), F32),
            vmem((31, 8, RANK), F32),
            vmem((2, 8, RANK), F32),
            vmem((7, 8, RANK), F32),
            vmem((2, 16, 8, RANK), F32),
            vmem((RANK, RANK), F32),
            vmem((RANK, RANK), F32),
            vmem((2, 4, HALF, RANK), F32),
            vmem((4, HALF, RANK), F32),
            vmem((4, HALF, RANK), F32),
            vmem((3, HALF, RANK), F32),
            dma((4,)),
            dma((SLOTS,)),
            dma((2,)),
            dma((2, 3)),
            dma((2, 3)),
            dma,
            dma((2, 2)),
            dma((2, 2)),
            dma((3, 2, 3)),
            dma((3, 2, 3)),
            dma((SLOTS, 2, 3)),
            dma((SLOTS, 2, 3)),
            dma,
            dma,
            dma((7,)),
            dma((7,)),
            dma,
            dma,
            dma,
            dma,
            dma((HALF // CHUNK,)),
            dma((HALF // CHUNK,)),
            dma((HALF // CHUNK, 3)),
            dma((HALF // CHUNK, 3)),
        ],
        compiler_params=pltpu.CompilerParams(
            collective_id=0, has_side_effects=True, vmem_limit_bytes=56 << 20
        ),
        cost_estimate=pl.CostEstimate(
            flops=3_300_000_000, bytes_accessed=12_000_000, transcendentals=0
        ),
    )(
        owner.reshape(SLOTS),
        sub_block,
        patient_block,
        live,
        tiles.reshape(SLOTS, BLOCK * MONTHS, BLOCK),
        code_factor,
        month_factor,
    )


def solution(mesh):
    placed = (
        P(("pat", "code"), None, None, None),
        P(("pat", "code")),
        P(("pat", "code"), None),
        P(("pat", "code")),
        P(("pat", "code")),
        P(("pat", "code"), None),
        P(),
    )
    return jax.shard_map(
        local, mesh=mesh, in_specs=placed, out_specs=P(("pat", "code"), None), check_vma=False
    )
```

```python
import jax
import jax.numpy as jnp
from jax import lax
from jax.experimental import pallas as pl
from jax.experimental.pallas import tpu as pltpu
from jax.sharding import PartitionSpec as P

MESH = pl.DeviceIdType.MESH
HI = lax.Precision.HIGHEST
F32 = jnp.float32
BLOCK = 128
MONTHS = 120
RANK = 256
SLOTS = 3
HALF = 64
CHUNK = 32
SIDE = 32


def recip(p):
    r = pltpu.reciprocal(p, approx=True)
    return r * (2.0 - p * r)


def tree(values, bits):
    while len(values) > 1:
        values = [
            jnp.where(bits[0], values[i + 1], values[i]) for i in range(0, len(values), 2)
        ]
        bits = bits[1:]
    return values[0]


def add_up(values):
    while len(values) > 1:
        values = [values[i] + values[i + 1] for i in range(0, len(values), 2)]
    return values[0]


def lane_of(v, at):
    return jnp.broadcast_to(v[:, at : at + 1], (8, 128))


def row_of(v, at):
    return jnp.broadcast_to(v[at : at + 1, :], (8, 128))


def sweep_pairs(d):
    n = 8

    def at(i, j):
        return d[min(i, j), max(i, j)]

    for k in range(0, n, 2):
        a, b, c = at(k, k), at(k, k + 1), at(k + 1, k + 1)
        r = recip(a * c - b * b)
        ia, ib, ic = c * r, b * r, a * r
        rest = [i for i in range(n) if i > k + 1] + [i for i in range(n) if i < k]
        u = {
            i: (ia * at(k, i) - ib * at(k + 1, i), ic * at(k + 1, i) - ib * at(k, i)) for i in rest
        }
        new = {}
        for p, i in enumerate(rest):
            for j in rest[p:]:
                new[min(i, j), max(i, j)] = at(i, j) - (at(k, i) * u[j][0] + at(k + 1, i) * u[j][1])
        for i in rest:
            new[min(i, k), max(i, k)] = u[i][0]
            new[min(i, k + 1), max(i, k + 1)] = u[i][1]
        new[k, k], new[k, k + 1], new[k + 1, k + 1] = -ia, ib, -ic
        d = new
    return d


def panel(rows, half, l0, row, lane, c):
    lines = [[row_of(rows[h], m) for m in range(8)] for h in range(2)]
    d = sweep_pairs({(i, j): row_of(c[j], i) for i in range(8) for j in range(i, 8)})
    row_bits = [(row & b) == b for b in (1, 2, 4)]
    rel = lane - l0
    lane_bits = [(rel & b) == b for b in (1, 2, 4)]
    minus = [tree([d[min(i, m), max(i, m)] for i in range(8)], row_bits) for m in range(8)]
    inside = -tree(minus, lane_bits)
    out = []
    for h in range(2):
        w = -add_up([minus[m] * lines[h][m] for m in range(8)])
        out.append(jnp.where((rel >= 0) & (rel < 8), inside, w) if h == half else w)
    return out, minus


def turned_dot(a, b):
    return lax.dot_general(
        a, b, (((0,), (0,)), ((), ())), precision=HI, preferred_element_type=F32
    )


def clear_and_subtract(a, s, rows, done):
    wide = lax.broadcasted_iota(jnp.int32, (1, RANK), 1)
    o = s * SIDE
    inside = (wide >= o) & (wide < o + SIDE)
    a[...] = jnp.where(inside, 0.0, a[...]) - turned_dot(rows, done)
    a[pl.ds(pl.multiple_of(jnp.maximum(o, 0), SIDE), SIDE), :] = done


def eliminate(a, first, last, carry, beside=None, after_step=None):
    row = lax.broadcasted_iota(jnp.int32, (8, 128), 0)
    lane = lax.broadcasted_iota(jnp.int32, (8, 128), 1)
    wide = lax.broadcasted_iota(jnp.int32, (1, RANK), 1)
    n = SIDE // 8

    def step(s, carry):
        turned, before, after = carry
        clear_and_subtract(a, s - 1, before, after)
        o = pl.multiple_of(s * SIDE, SIDE)
        ahead = pl.multiple_of(lax.rem(o + SIDE, RANK), SIDE)
        following = pltpu.roll(a[pl.ds(ahead, SIDE), :], RANK - o, 1)
        straight = pltpu.roll(turned, o, 1)
        rows = [[turned[8 * j : 8 * j + 8, :128], turned[8 * j : 8 * j + 8, 128:]] for j in range(n)]
        for j in range(n):
            l0 = 8 * j
            order = list(range(j + 1, n)) + list(range(j))
            factor = {i: [lane_of(rows[i][0], l0 + m) for m in range(8)] for i in order}
            if beside is not None and j == 1:
                beside(s)
            ahead_of_rows = beside is None and j + 1 < n
            if j == 0 or beside is not None:
                block = [lane_of(rows[j][0], l0 + m) for m in range(8)]
            if ahead_of_rows:
                later = [lane_of(rows[j + 1][0], l0 + 8 + m) for m in range(8)]
            rows[j], minus = panel(rows[j], 0, l0, row, lane, block)
            if ahead_of_rows:
                f = factor[j + 1]
                scaled = [add_up([minus[p] * row_of(f[p], m) for p in range(8)]) for m in range(8)]
                block = [
                    later[m] + add_up([f[q] * row_of(scaled[m], q) for q in range(8)])
                    for m in range(8)
                ]
            inside = (lane >= l0) & (lane < l0 + 8)
            w = [[row_of(rows[j][h], m) for m in range(8)] for h in range(2)]
            for i in order:
                for h in range(2):
                    old = jnp.where(inside, 0.0, rows[i][h]) if h == 0 else rows[i][h]
                    rows[i][h] = old - add_up([factor[i][m] * w[h][m] for m in range(8)])
        done = jnp.concatenate([jnp.concatenate(r, axis=1) for r in rows], axis=0)
        done = jnp.where(wide < SIDE, -done, done)
        following = jnp.where(wide < SIDE, 0.0, following) - turned_dot(
            turned[:, SIDE : 2 * SIDE], done
        )
        result = pltpu.roll(following, RANK - SIDE, 1), straight, pltpu.roll(done, o, 1)
        if after_step is not None:
            after_step(s)
        return result

    return lax.fori_loop(first, last, step, carry)


def far_first(offsets, hops):
    return sorted(offsets, key=hops, reverse=True)


RING = (0, 1, 2, 1)
PLANE = far_first(range(1, 32), lambda e: RING[e // 8] + RING[e // 2 % 4])
SPOTS = far_first(range(1, 16), lambda e: RING[e // 4] + RING[e % 4])
COLUMN = far_first(range(1, 8), lambda d: min(d, 8 - d))
LINE = (2, 1, 3)


def kernel(
    owner_in, sub_in, block_in, live_in, tiles, code_in, month_in, out, owner, sub, block_at, live,
    counts, code, month, group, need, need_in, asked, wanted, chosen, blocks,
    gram_own, plane_in, piece, column_in, whole, gram, month_gram,
    part, pair_in, line_out, line_in,
    scalar_sem, tile_sem, small_sem, need_s, need_r, asked_sem, zh_s, zh_r, row_s, row_r, pick_s, pick_r,
    plane_s, plane_r, column_s, column_r, spread_s, spread_r, halves_s, halves_r,
    pair_s, pair_r, line_s, line_r,
):
    pat, code_at = lax.axis_index("pat"), lax.axis_index("code")
    x, y, zh = pat // 8, (pat // 2) % 4, pat % 2
    zl, core = code_at // 2, code_at % 2
    z = zh * 4 + zl
    spot = x * 4 + y
    me = core * 16 + spot

    def device(x, y, z, c):
        x, y, z = lax.rem(x, 4), lax.rem(y, 4), lax.rem(z, 8)
        return ((x * 4 + y) * 2 + z // 4, lax.rem(z, 4) * 2 + c)

    def plane(e):
        px, py, pc = lax.rem(x + e // 8, 4), lax.rem(y + (e // 2) % 4, 4), core
        if e % 2:
            pc = 1 - core
        return device(px, py, z, pc), pc * 16 + px * 4 + py

    def beside(h, d):
        return device(x + d, y, z, core) if h == 0 else device(x, y + d, z, core)

    def remote(src, dst, send, recv, to):
        return pltpu.make_async_remote_copy(
            src_ref=src, dst_ref=dst, send_sem=send, recv_sem=recv, device_id=to, device_id_type=MESH
        )

    def start(copies):
        for c in copies:
            c.start()
        return copies

    def arrived(buf, sem):
        pltpu.make_async_copy(buf, buf, sem).wait()

    small = start(
        [
            pltpu.make_async_copy(code_in, code, small_sem.at[0]),
            pltpu.make_async_copy(month_in, month, small_sem.at[1]),
        ]
    )
    scalars = start(
        [
            pltpu.make_async_copy(src, dst, scalar_sem.at[n])
            for n, (src, dst) in enumerate(
                ((owner_in, owner), (sub_in, sub), (block_in, block_at), (live_in, live))
            )
        ]
    )
    barrier = pltpu.get_barrier_semaphore()

    for d in COLUMN:
        pl.semaphore_signal(
            barrier, inc=1, device_id=device(x, y, z + d, core), device_id_type=MESH
        )
    for e in PLANE:
        pl.semaphore_signal(barrier, inc=1, device_id=plane(e)[0], device_id_type=MESH)
    loads = start(
        [pltpu.make_async_copy(tiles.at[k], counts.at[k], tile_sem.at[k]) for k in range(SLOTS)]
    )
    for c in scalars:
        c.wait()
    line_at = lax.broadcasted_iota(jnp.int32, (8, 128), 0)
    places, away = [], []
    for k in range(SLOTS):
        o = owner[k]
        ox, oy, oz = o // 8, (o // 2) % 4, o % 2
        places.append([(oz * 4 + ox) * 2 + sub[k], (oz * 4 + oy) * 2 + sub[k]])
        away.append([lax.rem(y + 4 - oy, 4), lax.rem(x + 4 - ox, 4)])
    wish = jnp.zeros((8, 128), jnp.int32)
    for k in range(SLOTS):
        for h in range(2):
            wish = jnp.where(line_at == 2 * k + h, places[k][h], wish)
    need[...] = wish
    mine = [(zh * 4 + x) * 2, (zh * 4 + y) * 2]
    theirs = [((1 - zh) * 4 + x) * 2, ((1 - zh) * 4 + y) * 2]
    small[0].wait()
    for h in range(2):
        for b in range(2):
            group[h, mine[h] + b] = code[b * BLOCK : (b + 1) * BLOCK, h * BLOCK : (h + 1) * BLOCK]
    own = lax.dot_general(
        code[...], code[...], (((0,), (0,)), ((), ())), preferred_element_type=F32
    )
    gram_own[...] = own.reshape(32, 8, RANK)
    pl.semaphore_wait(barrier, 38)

    across = []
    for b in range(2):
        for h in range(2):
            here = group.at[h, mine[h] + b]
            across.append(remote(here, here, zh_s.at[b, h], zh_r.at[b, h], device(x, y, z + 4, core)))
    start(across)
    needs = start(
        [
            remote(need, need_in.at[h, d - 1], need_s.at[h, d - 1], need_r.at[h, d - 1], beside(1 - h, d))
            for h in range(2)
            for d in range(1, 4)
        ]
    )


    for e in PLANE:
        to, q = plane(e)
        remote(gram_own.at[q], plane_in.at[e - 1], plane_s, plane_r, to).start()

    def along_line(s, first, count):
        copies = []
        for h in range(2):
            here = group.at[h, pl.ds(first[h], count)]
            for d in LINE:
                copies.append(
                    remote(here, here, row_s.at[s, h, d - 1], row_r.at[s, h, d - 1], beside(h, d))
                )
        return start(copies)

    row_copies = along_line(0, mine, 2)
    small[1].wait()
    month_gram[...] = turned_dot(month[...], month[...])
    for c in needs:
        c.wait()
    to_scalars = pltpu.make_async_copy(need_in, asked, asked_sem)
    to_scalars.start()
    to_scalars.wait()
    for c in across[:2]:
        c.wait()
    row_copies = row_copies + along_line(1, theirs, 1)
    arrived(plane_in, plane_r)
    piece[0] = lax.fori_loop(0, 31, lambda e, t: t + plane_in[e], gram_own[me], unroll=True)
    columns = start(
        [
            remote(
                piece.at[0], column_in.at[d - 1], column_s.at[d - 1], column_r.at[d - 1],
                device(x, y, z + d, core),
            )
            for d in COLUMN
        ]
    )
    for c in across[2:]:
        c.wait()
    row_copies = row_copies + along_line(2, [t + 1 for t in theirs], 1)
    for c in columns:
        c.wait()
    total = piece[0]
    for d in range(7):
        total = total + column_in[d]
    piece[1] = total
    whole[core, spot] = total

    for e in SPOTS:
        to = device(x + e // 4, y + e % 4, z, core)
        remote(piece.at[1], whole.at[core, spot], spread_s, spread_r, to).start()
    for c in row_copies:
        c.wait()
    picks = []
    for k in range(SLOTS):
        for h in range(2):
            for d in LINE:
                wanted[k, h, d - 1] = group[h, asked[h, 3 - d, 2 * k + h, 0]]
                picks.append(
                    remote(
                        wanted.at[k, h, d - 1], chosen.at[k, h, d],
                        pick_s.at[k, h, d - 1], pick_r.at[k, h, d - 1], beside(1 - h, d),
                    )
                )
                picks[-1].start()
            chosen[k, h, 0] = group[h, places[k][h]]
    arrived(whole.at[0, 0:15], spread_r)
    halves = remote(
        whole.at[core], whole.at[core], halves_s, halves_r, device(x, y, z, 1 - core)
    )
    halves.start()
    halves.wait()
    gram[...] = whole[...].reshape(RANK, RANK) * month_gram[...]
    first = gram[0:SIDE, :]
    for c in picks:
        c.wait()
    for k in range(SLOTS):
        for h in range(2):
            blocks[k, :, h * BLOCK : (h + 1) * BLOCK] = chosen[k, h, away[k][h]]
    for load in loads:
        load.wait()

    per_half = HALF // CHUNK

    def contract(s):
        half = jnp.where(s < per_half, 1 - core, core)
        low = pl.multiple_of(lax.rem(s, per_half) * CHUNK, CHUNK)
        at = pl.multiple_of((half * HALF + low) * MONTHS, CHUNK * MONTHS)
        pieces = []
        for k in range(SLOTS):
            wide = jnp.dot(
                counts[k, pl.ds(at, CHUNK * MONTHS), :], blocks[k], preferred_element_type=F32
            )
            wide = wide.reshape(CHUNK, MONTHS, RANK) * month[...][None]
            pieces.append(jnp.sum(wide, axis=1) * live[k].astype(F32))
        for b in range(4):
            chosen_pieces = [jnp.where(block_at[k] == b, pieces[k], 0.0) for k in range(SLOTS)]
            part[half, b, pl.ds(low, CHUNK), :] = chosen_pieces[0] + chosen_pieces[1] + chosen_pieces[2]

    def pair_copy(n):
        at = pl.ds(pl.multiple_of(n * CHUNK, CHUNK), CHUNK)
        return remote(
            part.at[1 - core, :, at], pair_in.at[:, at], pair_s.at[n], pair_r.at[n],
            device(x, y, z, 1 - core),
        )

    def line_copy(n, d):
        at = pl.ds(pl.multiple_of(n * CHUNK, CHUNK), CHUNK)
        zt = lax.rem(zl + d, 4)
        return remote(
            line_out.at[zt, at], line_in.at[d - 1, at], line_s.at[n, d - 1], line_r.at[n, d - 1],
            device(x, y, zh * 4 + zt, core),
        )

    def send_sums(s):
        @pl.when(s < per_half)
        def _():
            pair_copy(s).start()

        @pl.when(s >= per_half)
        def _():
            n = s - per_half
            at = pl.ds(pl.multiple_of(n * CHUNK, CHUNK), CHUNK)
            pair_copy(n).wait()
            line_out[:, at] = part[core, :, at] + pair_in[:, at]
            for d in range(1, 4):
                line_copy(n, d).start()

    carry = (first, jnp.zeros_like(first), first)
    carry = eliminate(gram, 0, 2 * per_half, carry, contract, send_sums)
    line = [line_copy(n, d) for n in range(per_half) for d in range(1, 4)]
    _, before, after = eliminate(gram, 2 * per_half, RANK // SIDE, carry)
    for c in line:
        c.wait()
    share = line_out[zl] + line_in[0] + line_in[1] + line_in[2]
    kept = lax.broadcasted_iota(jnp.int32, (1, RANK), 1) < RANK - SIDE
    rest = jnp.where(kept, share, 0.0)
    main = jnp.dot(
        rest, jnp.where(kept, gram[...], 0.0), precision=HI, preferred_element_type=F32
    )
    last = share[:, RANK - SIDE :] - lax.dot_general(
        rest, before, (((1,), (1,)), ((), ())), precision=HI, preferred_element_type=F32
    )
    out[...] = -(main + jnp.dot(last, after, precision=HI, preferred_element_type=F32))
    arrived(gram_own.at[0:31], plane_s)
    arrived(gram_own.at[0:15], spread_s)


def local(tiles, patient_block, owner, sub_block, live, code_factor, month_factor):
    dma, vmem = pltpu.SemaphoreType.DMA, pltpu.VMEM
    vmem_spec = pl.BlockSpec(memory_space=pltpu.VMEM)
    return pl.pallas_call(
        kernel,
        out_shape=jax.ShapeDtypeStruct((HALF, RANK), F32),
        in_specs=[pl.BlockSpec(memory_space=pl.ANY)] * 7,
        out_specs=vmem_spec,
        scratch_shapes=[
            *[pltpu.SMEM((SLOTS,), jnp.int32)] * 4,
            vmem((SLOTS, BLOCK * MONTHS, BLOCK), jnp.bfloat16),
            vmem((2 * BLOCK, RANK), jnp.bfloat16),
            vmem((MONTHS, RANK), F32),
            vmem((2, 16, BLOCK, BLOCK), jnp.bfloat16),
            vmem((8, 128), jnp.int32),
            vmem((2, 3, 8, 128), jnp.int32),
            pltpu.SMEM((2, 3, 8, 128), jnp.int32),
            vmem((SLOTS, 2, 3, BLOCK, BLOCK), jnp.bfloat16),
            vmem((SLOTS, 2, 4, BLOCK, BLOCK), jnp.bfloat16),
            vmem((SLOTS, BLOCK, RANK), jnp.bfloat16),
            vmem((32, 8, RANK), F32),
            vmem((31, 8, RANK), F32),
            vmem((2, 8, RANK), F32),
            vmem((7, 8, RANK), F32),
            vmem((2, 16, 8, RANK), F32),
            vmem((RANK, RANK), F32),
            vmem((RANK, RANK), F32),
            vmem((2, 4, HALF, RANK), F32),
            vmem((4, HALF, RANK), F32),
            vmem((4, HALF, RANK), F32),
            vmem((3, HALF, RANK), F32),
            dma((4,)),
            dma((SLOTS,)),
            dma((2,)),
            dma((2, 3)),
            dma((2, 3)),
            dma,
            dma((2, 2)),
            dma((2, 2)),
            dma((3, 2, 3)),
            dma((3, 2, 3)),
            dma((SLOTS, 2, 3)),
            dma((SLOTS, 2, 3)),
            dma,
            dma,
            dma((7,)),
            dma((7,)),
            dma,
            dma,
            dma,
            dma,
            dma((HALF // CHUNK,)),
            dma((HALF // CHUNK,)),
            dma((HALF // CHUNK, 3)),
            dma((HALF // CHUNK, 3)),
        ],
        compiler_params=pltpu.CompilerParams(
            collective_id=0, has_side_effects=True, vmem_limit_bytes=56 << 20
        ),
        cost_estimate=pl.CostEstimate(
            flops=3_300_000_000, bytes_accessed=12_000_000, transcendentals=0
        ),
    )(
        owner.reshape(SLOTS),
        sub_block,
        patient_block,
        live,
        tiles.reshape(SLOTS, BLOCK * MONTHS, BLOCK),
        code_factor,
        month_factor,
    )


def solution(mesh):
    placed = (
        P(("pat", "code"), None, None, None),
        P(("pat", "code")),
        P(("pat", "code"), None),
        P(("pat", "code")),
        P(("pat", "code")),
        P(("pat", "code"), None),
        P(),
    )
    return jax.shard_map(
        local, mesh=mesh, in_specs=placed, out_specs=P(("pat", "code"), None), check_vma=False
    )
```
